32 devices in a mesh: groups: 2 (over y), gx: 4 (over z), gy: 2 (over x), col: 2 (over core).
Axes of the slice: x: 2, y: 2, z: 4, core: 2. Of those that a mesh axis runs over, the one named last changes fastest.
Arguments:
- state_in: bfloat16 [64, 2048, 2048], P(('groups', 'col'), 'gx', 'gy'), parts along dimension 0, may hold values from -6 to 6
- tile_class: int32 [256, 128], P(('groups', 'gx'), 'gy'), parts along dimension 0, may hold values from 0 to 7
- class_bias: float32 [8, 32], replicated, may hold values from -4 to 4
- w_point: bfloat16 [32, 32], replicated, may hold values from -1 to 1
- spec_weight: bfloat16 [2, 32, 32, 128, 128], P(None, None, 'col', 'gx', 'gy'), may hold values from -0.75 to 0.75
- grad_out: bfloat16 [64, 2048, 2048], P(('groups', 'col'), 'gx', 'gy'), parts along dimension 0, may hold values from -6 to 6
Outputs:
- act_out: bfloat16 [64, 2048, 2048], P(('groups', 'col'), 'gx', 'gy'), parts along dimension 0
- grad_in: bfloat16 [64, 2048, 2048], P(('groups', 'col'), 'gx', 'gy'), parts along dimension 0
- grad_spec: float32 [4, 32, 32, 128, 128], P('groups', None, 'col', 'gx', 'gy'), parts along dimension 0
- grad_point: float32 [64, 32], P(('groups', 'col')), parts along dimension 0
- grad_bias: float32 [16, 32], P('groups', 'col'), parts along dimension 0
The draws below stay inside these ranges and needn't reach their ends.
There are 2 independent parts, one for each index of `groups`. The reference program is written for one: setup_inputs(seed, part) draws one part's arguments, and reference() takes and returns one part's arrays. A program takes and returns all parts, laid end to end along the dimension named above; an argument that names none is the same for every part. Nothing has to cross between parts.
Inputs may be any that keep to these rules, and one draw needn't show every extreme that they name: `tile_class`: bathymetry class of each 16 x 16 tile of cells.
All inputs are finite; a program needn't handle non-finite values.
Results may differ from the reference program's by a relative error of at most 0.015.
Values may be sent and summed in bfloat16 or wider, within the bound.
A program may use at most 640 MiB of HBM per device.

```python
import math
import jax
import jax.numpy as jnp
from jax import lax

C = 32
NX = 2048
NY = 2048
MX = 128
MY = 128
TILE = 16
NCLASS = 8
N_GY = 2


def plant(result, stream_key, smallest, largest):
    longest = result.shape.index(max(result.shape))
    spots = []
    for shift in (0, 1):
        where = [jax.random.randint(jax.random.fold_in(stream_key, axis), (), 0, length) for axis, length in enumerate(result.shape)]
        where[longest] = (where[longest] + shift) % result.shape[longest]
        spots.append(tuple(where))
    return result.at[spots[0]].set(smallest).at[spots[1]].set(largest)


def level_of(own_key, extent, cuts, low, largest):
    gain, own = 1.0, jax.random.fold_in(own_key, 6)
    for position, blocks in cuts:
        draws = jnp.exp(jax.random.uniform(jax.random.fold_in(own, position), (blocks,), jnp.float32, low / len(cuts), largest / len(cuts)))
        gain = gain * jnp.repeat(draws, extent[position] // blocks).reshape([-1 if axis == position else 1 for axis in range(len(extent))])
    return gain


def gaussian(key, shape, deviation, bound, split=(), kind=jnp.bfloat16):
    drawn = deviation * jax.random.normal(key, shape, jnp.float32)
    if split:
        drawn = drawn * level_of(key, shape, split, -0.22, 0.18)
    return jnp.clip(drawn, -bound, bound).astype(kind)


def setup_inputs(seed: int = 0, part: int = 0) -> dict:
    keys = jax.random.split(jax.random.key(seed), 7)
    part_splits = jax.random.split(jax.random.fold_in(keys[6], part), 7)
    return {
        "state_in": gaussian(part_splits[0], (C, NX, NY), 1.0, 6.0, ((0, 2), (1, 4), (2, 2))),
        "tile_class": plant(jax.random.randint(part_splits[1], (NX // TILE, NY // TILE), 0, NCLASS), jax.random.fold_in(part_splits[1], 1), 0, NCLASS - 1).astype(jnp.int32),
        "class_bias": gaussian(keys[2], (NCLASS, C), 1.0, 4.0, (), jnp.float32),
        "w_point": gaussian(keys[3], (C, C), C ** -0.5, 1.0),
        "spec_weight": gaussian(keys[4], (2, C, C, MY, MX), (2 * C) ** -0.5, 0.75, ((2, 2), (3, 4), (4, 2))),
        "grad_out": gaussian(part_splits[5], (C, NX, NY), 1.0, 6.0, ((0, 2), (1, 4), (2, 2))),
    }


root_half = 0.7071067811865476
inv_root_tau = 0.3989422804014327

def make_tables():
    freq_y = jnp.arange(MY, dtype=jnp.int32)
    points_y = jnp.arange(NY, dtype=jnp.int32)
    angles_y = (points_y[:, None] * freq_y[None, :] % NY).astype(jnp.float32) * (2.0 * math.pi / NY)
    y_fwd = jnp.stack([jnp.cos(angles_y), -jnp.sin(angles_y)]).astype(jnp.bfloat16)
    angles_t = (freq_y[:, None] * points_y[None, :] % NY).astype(jnp.float32) * (2.0 * math.pi / NY)
    weight_k = jnp.where(freq_y == 0, 1.0, 2.0).astype(jnp.float32)[:, None]
    y_inv = jnp.stack([weight_k * jnp.cos(angles_t), -weight_k * jnp.sin(angles_t)]).astype(jnp.bfloat16)
    freq_x = jnp.arange(MX, dtype=jnp.int32)
    signed_x = jnp.where(freq_x < MX // 2, freq_x, freq_x - MX)
    points_x = jnp.arange(NX, dtype=jnp.int32)
    angles_x = (signed_x[:, None] * points_x[None, :] % NX).astype(jnp.float32) * (2.0 * math.pi / NX)
    cos_part = jnp.cos(angles_x)
    sin_part = jnp.sin(angles_x)
    x_fwd = jnp.stack([jnp.stack([cos_part, -sin_part]), jnp.stack([sin_part, cos_part])]).astype(jnp.bfloat16)
    x_inv = jnp.stack([jnp.stack([cos_part, sin_part]), jnp.stack([-sin_part, cos_part])]).astype(jnp.bfloat16)
    return (y_fwd, y_inv, x_fwd, x_inv)

def mix_modes(weight, spectrum):
    high = lax.Precision.HIGHEST
    real_part = jnp.einsum('iokm,ikm->okm', weight[0], spectrum[0], precision=high) - jnp.einsum('iokm,ikm->okm', weight[1], spectrum[1], precision=high)
    imag_part = jnp.einsum('iokm,ikm->okm', weight[0], spectrum[1], precision=high) + jnp.einsum('iokm,ikm->okm', weight[1], spectrum[0], precision=high)
    return jnp.stack([real_part, imag_part])

def back_mix(weight, grad_modes):
    high = lax.Precision.HIGHEST
    real_part = jnp.einsum('iokm,okm->ikm', weight[0], grad_modes[0], precision=high) + jnp.einsum('iokm,okm->ikm', weight[1], grad_modes[1], precision=high)
    imag_part = jnp.einsum('iokm,okm->ikm', weight[0], grad_modes[1], precision=high) - jnp.einsum('iokm,okm->ikm', weight[1], grad_modes[0], precision=high)
    return jnp.stack([real_part, imag_part])

def weight_grad(spectrum, grad_modes):
    real_part = jnp.einsum('ikm,okm->iokm', spectrum[0], grad_modes[0]) + jnp.einsum('ikm,okm->iokm', spectrum[1], grad_modes[1])
    imag_part = jnp.einsum('ikm,okm->iokm', spectrum[0], grad_modes[1]) - jnp.einsum('ikm,okm->iokm', spectrum[1], grad_modes[0])
    return jnp.stack([real_part, imag_part])

def reference(state_in, tile_class, class_bias, w_point, spec_weight, grad_out):
    y_fwd, y_inv, x_fwd, x_inv = make_tables()
    y_fwd_f = y_fwd.astype(jnp.float32)
    y_inv_f = y_inv.astype(jnp.float32)
    x_fwd_f = x_fwd.astype(jnp.float32)
    x_inv_f = x_inv.astype(jnp.float32)
    scale_fwd = 1.0 / math.sqrt(NX * NY)
    scale_inv = 1.0 / math.sqrt(2.0 * MX * MY)
    state_f = state_in.astype(jnp.float32)
    w_float = w_point.astype(jnp.float32)
    point_mix = jnp.einsum('oi,ixy->oxy', w_float, state_f)
    block_cols = NY // N_GY
    spectrum = jnp.zeros((2, C, MY, MX), jnp.float32)
    for block in range(N_GY):
        lower = block * block_cols
        row_spec = jnp.einsum('cxy,tyk->tckx', state_f[:, :, lower:lower + block_cols], y_fwd_f[:, lower:lower + block_cols]).astype(jnp.bfloat16)
        spectrum = spectrum + jnp.einsum('rckx,rtmx->tckm', row_spec.astype(jnp.float32), x_fwd_f)
    spectrum = spectrum * scale_fwd
    weight_f = spec_weight.astype(jnp.float32)
    mixed = mix_modes(weight_f, spectrum).astype(jnp.bfloat16)
    space_rows = jnp.einsum('rokm,rtmx->tokx', mixed.astype(jnp.float32), x_inv_f).astype(jnp.bfloat16)
    spectral = scale_inv * jnp.einsum('tokx,tky->oxy', space_rows.astype(jnp.float32), y_inv_f)
    one_hot = (tile_class[:, :, None] == jnp.arange(NCLASS, dtype=jnp.int32)).astype(jnp.float32)
    tile_bias = jnp.einsum('abn,no->oab', one_hot, class_bias.astype(jnp.float32))
    tile_rows = NX // TILE
    tile_cols = NY // TILE
    summed = (point_mix + spectral).reshape(C, tile_rows, TILE, tile_cols, TILE)
    pre_act = (summed + tile_bias[:, :, None, :, None]).reshape(C, NX, NY)
    normal_cdf = 0.5 * (1.0 + jax.scipy.special.erf(pre_act * root_half))
    act_out = (pre_act * normal_cdf).astype(jnp.bfloat16)
    gelu_slope = normal_cdf + pre_act * jnp.exp(-0.5 * pre_act * pre_act) * inv_root_tau
    grad_pre = (grad_out.astype(jnp.float32) * gelu_slope).astype(jnp.bfloat16)
    grad_float = grad_pre.astype(jnp.float32)
    grad_point = scale_fwd * jnp.einsum('oxy,ixy->oi', grad_float, state_f)
    tile_sums = grad_float.reshape(C, tile_rows, TILE, tile_cols, TILE).sum(axis=(2, 4))
    grad_bias = scale_fwd * jnp.einsum('abn,oab->no', one_hot, tile_sums)
    grad_modes = jnp.zeros((2, C, MY, MX), jnp.float32)
    for block in range(N_GY):
        lower = block * block_cols
        grad_rows = (scale_inv * jnp.einsum('oxy,tky->tokx', grad_float[:, :, lower:lower + block_cols], y_inv_f[:, :, lower:lower + block_cols])).astype(jnp.bfloat16)
        grad_modes = grad_modes + jnp.einsum('tokx,rtmx->rokm', grad_rows.astype(jnp.float32), x_inv_f)
    grad_spec = weight_grad(spectrum, grad_modes)
    input_modes = back_mix(weight_f, grad_modes).astype(jnp.bfloat16)
    input_rows = (scale_fwd * jnp.einsum('tckm,rtmx->rckx', input_modes.astype(jnp.float32), x_fwd_f)).astype(jnp.bfloat16)
    grad_in = jnp.einsum('oi,oxy->ixy', w_float, grad_float) + jnp.einsum('rckx,ryk->cxy', input_rows.astype(jnp.float32), y_fwd_f)
    return (act_out, grad_in.astype(jnp.bfloat16), grad_spec, grad_point, grad_bias)
```

```python
import functools
import math

import jax
import jax.numpy as jnp
import numpy as np
from jax import lax
from jax.experimental import pallas as pl
from jax.experimental.pallas import tpu as pltpu
from jax.sharding import PartitionSpec as P

NX = 2048
NY = 2048
MX = 128
MY = 128
TILE = 16
NCLASS = 8

SCALE_FWD = 1.0 / math.sqrt(NX * NY)
SCALE_INV = 1.0 / math.sqrt(2.0 * MX * MY)
root_half = 0.7071067811865476
inv_root_tau = 0.3989422804014327

NN = (((1,), (0,)), ((), ()))
NT = (((1,), (1,)), ((), ()))
VMEM_LIMIT = 50 * 1024 * 1024


def host_tables():
    freq_y = np.arange(MY)
    angles = (freq_y[:, None] * np.arange(NY)[None, :] % NY).astype(np.float32)
    angles = angles * np.float32(2.0 * math.pi / NY)
    y_table = np.concatenate([np.cos(angles), -np.sin(angles)]).astype(jnp.bfloat16)
    freq_x = np.arange(MX)
    signed = np.where(freq_x < MX // 2, freq_x, freq_x - MX)
    angles = (np.arange(NX)[:, None] * signed[None, :] % NX).astype(np.float32)
    angles = angles * np.float32(2.0 * math.pi / NX)
    x_table = np.concatenate([np.cos(angles), np.sin(angles)], axis=1).astype(jnp.bfloat16)
    return y_table, x_table


def dot(a, b, dims=NN):
    return lax.dot_general(a, b, dims, preferred_element_type=jnp.float32)


def fwd_kernel(state_ref, y_ref, x_ref, out_ref):
    rows_t = dot(y_ref[...], state_ref[0], NT).astype(jnp.bfloat16)
    full = dot(rows_t, x_ref[...])
    out_ref[0, 0] = (full[:MY, :MX] + full[MY:, MX:]).astype(jnp.bfloat16)
    out_ref[1, 0] = (full[MY:, :MX] - full[:MY, MX:]).astype(jnp.bfloat16)


def expand_modes(modes_ref, x_ref, rows_scr, scale):
    cos, sin = x_ref[:, :MX], x_ref[:, MX:]
    left = (jnp.concatenate([cos, -sin], 1), jnp.concatenate([sin, cos], 1))

    def pair(p, carry):
        both = jnp.concatenate(
            [modes_ref[t, pl.ds(2 * p, 2)].reshape(2 * MY, MX) for t in range(2)], 1
        )
        for t in range(2):
            res = dot(left[t], both, NT) * scale
            for s in range(2):
                rows_scr[2 * p + s, :, t * MY:(t + 1) * MY] = res[
                    :, s * MY:(s + 1) * MY
                ].astype(jnp.bfloat16)
        return carry

    lax.fori_loop(0, rows_scr.shape[0] // 2, pair, 0)


def lane_weight():
    lane = lax.broadcasted_iota(jnp.int32, (1, 2 * MY), 1)
    return jnp.where(lane % MY == 0, SCALE_INV, 2.0 * SCALE_INV).astype(jnp.float32)


def gelu_parts(v):
    cdf = 0.5 + 0.5 * lax.erf(v * root_half)
    bell = jnp.exp(v * v * -0.5)
    return v * cdf, cdf + v * bell * inv_root_tau


def mid_kernel(state_ref, gout_ref, modes_ref, kron_ref, y_ref, x_ref, xt_ref, bias_ref,
               hot_ref, act_ref, gpre_ref, terms_ref, rows_scr, g_scr):
    step = pl.program_id(0)
    chans = gout_ref.shape[0]
    cols = gout_ref.shape[2]
    chunk = min(256, cols)

    @pl.when(step == 0)
    def _():
        expand_modes(modes_ref, x_ref, rows_scr, lane_weight())

    here = pl.ds(pl.multiple_of(step * TILE, TILE), TILE)
    rows = rows_scr[:, here, :].reshape(chans * TILE, 2 * MY)
    total = None
    for j in range(cols // chunk):
        lanes = slice(j * chunk, (j + 1) * chunk)
        cells = state_ref[:, :, lanes].reshape(-1, chunk)
        table = y_ref[:, lanes]
        pre = dot(kron_ref[...], cells) + dot(rows, table)
        bias = dot(bias_ref[...], hot_ref[0, :, lanes])
        parts = []
        for o in range(chans):
            v = pre[o * TILE:(o + 1) * TILE] + bias[o:o + 1]
            act, slope = gelu_parts(v)
            act_ref[o, :, lanes] = act.astype(jnp.bfloat16)
            grad = (gout_ref[o, :, lanes].astype(jnp.float32) * slope).astype(jnp.bfloat16)
            gpre_ref[o, :, lanes] = grad
            parts.append(grad)
        term = dot(jnp.concatenate(parts, 0), table, NT)
        total = term if total is None else total + term
    g_scr[:, here, :] = (total * lane_weight()).astype(jnp.bfloat16).reshape(chans, TILE, 2 * MY)

    @pl.when(step == pl.num_programs(0) - 1)
    def _():
        def one(o, carry):
            full = dot(xt_ref[...], g_scr[o])
            real = full[:MX, :MY] + full[MX:, MY:]
            imag = full[:MX, MY:] - full[MX:, :MY]
            terms_ref[0, o] = real.T.astype(jnp.bfloat16)
            terms_ref[1, o] = imag.T.astype(jnp.bfloat16)
            return carry

        lax.fori_loop(0, chans, one, 0)


def sums_kernel(state_ref, gpre_ref, hot_ref, point_ref, bias_ref, acc, acc_b):
    step = pl.program_id(0)
    chans, tile, cols = gpre_ref.shape
    every = state_ref.shape[0]

    @pl.when(step == 0)
    def _():
        acc[...] = jnp.zeros_like(acc)
        acc_b[...] = jnp.zeros_like(acc_b)

    grad = gpre_ref[...]
    acc[...] += dot(grad.reshape(chans * tile, cols), state_ref[...].reshape(every * tile, cols), NT)
    col = grad.astype(jnp.float32).sum(axis=1)
    high = col.astype(jnp.bfloat16)
    low = (col - high.astype(jnp.float32)).astype(jnp.bfloat16)
    acc_b[...] += dot(high, hot_ref[0], NT) + dot(low, hot_ref[0], NT)

    @pl.when(step == pl.num_programs(0) - 1)
    def _():
        shape = (chans * tile, every * tile)
        row = lax.broadcasted_iota(jnp.int32, shape, 0) % tile
        lane = lax.broadcasted_iota(jnp.int32, shape, 1) % tile
        kept = jnp.where(row == lane, acc[...], 0.0)
        group = lax.broadcasted_iota(jnp.int32, (every * tile, every), 0) // tile
        which = lax.broadcasted_iota(jnp.int32, (every * tile, every), 1)
        ones = (group == which).astype(jnp.float32)
        summed = lax.dot_general(kept, ones, NN, precision=lax.Precision.HIGHEST,
                                 preferred_element_type=jnp.float32)
        point_ref[...] = summed.reshape(chans, tile, every).sum(axis=1) * SCALE_FWD
        bias_ref[...] = acc_b[...] * SCALE_FWD


def back_kernel(grad_ref, modes_ref, kron_ref, y_ref, x_ref, out_ref, rows_scr):
    step = pl.program_id(0)
    chans, tile, cols = out_ref.shape
    chunk = min(256, cols)

    @pl.when(step == 0)
    def _():
        expand_modes(modes_ref, x_ref, rows_scr, SCALE_FWD)

    here = pl.ds(pl.multiple_of(step * TILE, TILE), TILE)
    rows = rows_scr[:, here, :].reshape(chans * TILE, 2 * MY)
    for j in range(cols // chunk):
        lanes = slice(j * chunk, (j + 1) * chunk)
        cells = grad_ref[:, :, lanes].reshape(-1, chunk)
        res = dot(kron_ref[...], cells) + dot(rows, y_ref[:, lanes])
        out_ref[:, :, lanes] = res.astype(jnp.bfloat16).reshape(chans, tile, chunk)


def whole(array):
    return pl.BlockSpec(array.shape, lambda *_: (0,) * array.ndim)


def call(kernel, name, grid, in_specs, out_specs, out_shape, scratch, cost):
    return pl.pallas_call(
        kernel, grid=grid, in_specs=in_specs, out_specs=out_specs, out_shape=out_shape,
        scratch_shapes=scratch, name=name,
        compiler_params=pltpu.CompilerParams(
            dimension_semantics=("arbitrary",), vmem_limit_bytes=VMEM_LIMIT
        ),
        cost_estimate=pl.CostEstimate(flops=cost[0], bytes_accessed=cost[1], transcendentals=0),
    )


def mix_modes(weight, spectrum):
    real_part = jnp.einsum("iokm,ikm->okm", weight[0], spectrum[0], precision="highest") - jnp.einsum(
        "iokm,ikm->okm", weight[1], spectrum[1], precision="highest"
    )
    imag_part = jnp.einsum("iokm,ikm->okm", weight[0], spectrum[1], precision="highest") + jnp.einsum(
        "iokm,ikm->okm", weight[1], spectrum[0], precision="highest"
    )
    return jnp.stack([real_part, imag_part])


def back_mix(weight, grad_modes):
    real_part = jnp.einsum("iokm,okm->ikm", weight[0], grad_modes[0], precision="highest") + jnp.einsum(
        "iokm,okm->ikm", weight[1], grad_modes[1], precision="highest"
    )
    imag_part = jnp.einsum("iokm,okm->ikm", weight[0], grad_modes[1], precision="highest") - jnp.einsum(
        "iokm,okm->ikm", weight[1], grad_modes[0], precision="highest"
    )
    return jnp.stack([real_part, imag_part])


def weight_grad(spectrum, grad_modes):
    s = spectrum[:, :, None]
    g = grad_modes[:, None]
    return jnp.stack([s[0] * g[0] + s[1] * g[1], s[0] * g[1] - s[1] * g[0]])


def scatter_sum(terms, n_gx, n_gy):
    two, chans = terms.shape[:2]
    own_k, own_m = MY // n_gx, MX // n_gy
    blocks = terms.reshape(two, chans, n_gx, own_k, n_gy, own_m).transpose(2, 4, 0, 1, 3, 5)
    blocks = blocks.reshape(n_gx * n_gy, two, chans, own_k, own_m)
    got = lax.all_to_all(blocks, ("gx", "gy"), split_axis=0, concat_axis=0, tiled=True)
    return got.astype(jnp.float32).sum(axis=0)


def gather_modes(modes):
    along = lax.all_gather(modes, "gy", axis=3, tiled=True)
    return lax.all_gather(along, "gx", axis=2, tiled=True)


def on_device(n_gx, n_gy, state_in, tile_class, class_bias, w_point, spec_weight, grad_out):
    chans, rows, cols = state_in.shape
    every = w_point.shape[0]
    gx_index = lax.axis_index("gx")
    gy_index = lax.axis_index("gy")
    col_index = lax.axis_index("col")
    bf16 = jnp.bfloat16
    y_all, x_all = host_tables()
    y_table = lax.dynamic_slice_in_dim(jnp.asarray(y_all), gy_index * cols, cols, 1)
    x_table = lax.dynamic_slice_in_dim(jnp.asarray(x_all), gx_index * rows, rows, 0)
    x_table_t = lax.dynamic_slice_in_dim(jnp.asarray(x_all.T.copy()), gx_index * rows, rows, 1)
    state_all = lax.all_gather(state_in, "col", axis=0, tiled=True)
    w_rows = lax.dynamic_slice_in_dim(w_point, col_index * chans, chans, 0)
    w_cols = lax.dynamic_slice_in_dim(w_point, col_index * chans, chans, 1)
    same = jnp.eye(TILE, dtype=bf16)
    kron_fwd = (w_rows[:, None, :, None] * same[None, :, None, :]).reshape(chans * TILE, every * TILE)
    kron_bwd = (w_cols.T[:, None, :, None] * same[None, :, None, :]).reshape(
        chans * TILE, every * TILE
    )
    hot = (
        jnp.repeat(tile_class, TILE, axis=1)[:, None, :]
        == (jnp.arange(2 * NCLASS, dtype=jnp.int32) % NCLASS)[None, :, None]
    ).astype(bf16)
    bias_own = lax.dynamic_slice_in_dim(class_bias, col_index * chans, chans, 1).T
    bias_high = bias_own.astype(bf16)
    bias_low = (bias_own - bias_high.astype(jnp.float32)).astype(bf16)
    bias_pair = jnp.concatenate([bias_high, bias_low], 1)

    steps = rows // TILE
    cells = rows * cols
    wide = 2 * MY
    block = pl.BlockSpec((chans, TILE, cols), lambda b: (0, b, 0))
    block_all = pl.BlockSpec((every, TILE, cols), lambda b: (0, b, 0))
    block_hot = pl.BlockSpec((1, 2 * NCLASS, cols), lambda b: (b, 0, 0))
    modes_shape = jax.ShapeDtypeStruct((2, chans, MY, MX), bf16)
    field_shape = jax.ShapeDtypeStruct((chans, rows, cols), bf16)
    rows_scratch = pltpu.VMEM((chans, rows, wide), bf16)

    terms = call(
        fwd_kernel, "forward_transform", (chans,),
        [pl.BlockSpec((1, rows, cols), lambda c: (c, 0, 0)), whole(y_table), whole(x_table)],
        pl.BlockSpec((2, 1, MY, MX), lambda c: (0, c, 0, 0)),
        modes_shape, [], (2 * chans * cells * wide, 2 * chans * cells),
    )(state_in, y_table, x_table)
    spectrum = scatter_sum(terms, n_gx, n_gy) * SCALE_FWD
    spec_all = lax.all_gather(spectrum, "col", axis=1, tiled=True)
    weight_f = spec_weight.astype(jnp.float32)
    mixed = mix_modes(weight_f, spec_all).astype(bf16)
    mixed_all = gather_modes(mixed)

    act_out, grad_pre, grad_terms = call(
        mid_kernel, "layer_and_adjoint", (steps,),
        [block_all, block, whole(modes_shape), whole(kron_fwd), whole(y_table), whole(x_table),
         whole(x_table_t), whole(bias_pair), block_hot],
        [block, block, whole(modes_shape)],
        [field_shape, field_shape, modes_shape],
        [rows_scratch, rows_scratch],
        (2 * chans * cells * (2 * wide + every * TILE), 10 * chans * cells),
    )(state_all, grad_out, mixed_all, kron_fwd, y_table, x_table, x_table_t, bias_pair, hot)

    grad_all = lax.all_gather(grad_pre, "col", axis=0, tiled=True)
    point_sum, bias_sum = call(
        sums_kernel, "weight_sums", (steps,), [block_all, block, block_hot],
        [pl.BlockSpec((chans, every), lambda b: (0, 0)),
         pl.BlockSpec((chans, 2 * NCLASS), lambda b: (0, 0))],
        [jax.ShapeDtypeStruct((chans, every), jnp.float32),
         jax.ShapeDtypeStruct((chans, 2 * NCLASS), jnp.float32)],
        [pltpu.VMEM((chans * TILE, every * TILE), jnp.float32),
         pltpu.VMEM((chans, 2 * NCLASS), jnp.float32)],
        (2 * chans * cells * every * TILE, 6 * chans * cells),
    )(state_all, grad_pre, hot)
    sums = jnp.concatenate([point_sum, bias_sum], 1)
    sums = lax.all_gather(sums, ("gx", "gy"), axis=0, tiled=False).sum(axis=0)
    point_grad = sums[:, :every]
    bias_grad = sums[:, every:every + NCLASS].T

    grad_modes = scatter_sum(grad_terms, n_gx, n_gy)
    input_terms = back_mix(weight_f, grad_modes)
    input_modes = lax.psum_scatter(input_terms, "col", scatter_dimension=1, tiled=True).astype(bf16)
    input_all = gather_modes(input_modes)
    spec_grad = weight_grad(spec_all, grad_modes)

    grad_in = call(
        back_kernel, "input_gradient", (steps,),
        [block_all, whole(modes_shape), whole(kron_bwd), whole(y_table), whole(x_table)],
        block, field_shape, [rows_scratch],
        (2 * chans * cells * (wide + every * TILE), 6 * chans * cells),
    )(grad_all, input_all, kron_bwd, y_table, x_table)
    return (act_out, grad_in, spec_grad, point_grad, bias_grad)


def solution(mesh):
    return jax.shard_map(
        functools.partial(on_device, mesh.shape["gx"], mesh.shape["gy"]),
        mesh=mesh,
        in_specs=(
            P(("groups", "col"), "gx", "gy"),
            P(("groups", "gx"), "gy"),
            P(),
            P(),
            P(None, None, "col", "gx", "gy"),
            P(("groups", "col"), "gx", "gy"),
        ),
        out_specs=(
            P(("groups", "col"), "gx", "gy"),
            P(("groups", "col"), "gx", "gy"),
            P("groups", None, "col", "gx", "gy"),
            P(("groups", "col"), None),
            P("groups", "col"),
        ),
        check_vma=False,
    )
```

```python
import functools
import math

import jax
import jax.numpy as jnp
import numpy as np
from jax import lax
from jax.experimental import pallas as pl
from jax.experimental.pallas import tpu as pltpu
from jax.sharding import PartitionSpec as P

NX = 2048
NY = 2048
MX = 128
MY = 128
TILE = 16
NCLASS = 8

SCALE_FWD = 1.0 / math.sqrt(NX * NY)
SCALE_INV = 1.0 / math.sqrt(2.0 * MX * MY)
root_half = 0.7071067811865476
inv_root_tau = 0.3989422804014327

NN = (((1,), (0,)), ((), ()))
NT = (((1,), (1,)), ((), ()))
VMEM_LIMIT = 50 * 1024 * 1024


def host_tables(n_gy):
    freq_y = np.arange(MY)
    angles = (freq_y[:, None] * np.arange(NY)[None, :] % NY).astype(np.float32)
    angles = angles * np.float32(2.0 * math.pi / NY)
    y_table = np.concatenate([np.cos(angles), -np.sin(angles)]).astype(jnp.bfloat16)
    freq_x = np.arange(MX)
    signed = np.where(freq_x < MX // 2, freq_x, freq_x - MX)
    angles = (np.arange(NX)[:, None] * signed[None, :] % NX).astype(np.float32)
    angles = angles * np.float32(2.0 * math.pi / NX)
    cos, sin = (f(angles).reshape(NX, n_gy, 1, MX // n_gy) for f in (np.cos, np.sin))
    x_table = np.stack([np.concatenate([cos, -sin], 2), np.concatenate([sin, cos], 2)])
    return y_table, x_table.reshape(2, NX, 2 * MX).astype(jnp.bfloat16)


def dot(a, b, dims=NN):
    return lax.dot_general(a, b, dims, preferred_element_type=jnp.float32)


def fwd_kernel(state_ref, y_ref, x_ref, out_ref):
    rows_t = dot(y_ref[...], state_ref[0], NT).astype(jnp.bfloat16)
    full = dot(rows_t[:MY], x_ref[0]) + dot(rows_t[MY:], x_ref[1])
    wide = out_ref.shape[-1]
    for g in range(out_ref.shape[0]):
        out_ref[g, 0] = full[:, g * wide:(g + 1) * wide].astype(jnp.bfloat16)


def expand_modes(modes_ref, x_ref, rows_scr, scale):
    n_gy, wide = modes_ref.shape[0], modes_ref.shape[3]

    def pair(p, carry):
        parts = [modes_ref[g, pl.ds(2 * p, 2)].reshape(2 * MY, wide) for g in range(n_gy)]
        for t in range(2):
            if wide % 128 == 0:
                res = dot(x_ref[t], jnp.concatenate(parts, 1), NT)
            else:
                res = sum(
                    dot(x_ref[t, :, g * wide:(g + 1) * wide], parts[g], NT) for g in range(n_gy)
                )
            res = res * scale
            for s in range(2):
                rows_scr[2 * p + s, :, t * MY:(t + 1) * MY] = res[
                    :, s * MY:(s + 1) * MY
                ].astype(jnp.bfloat16)
        return carry

    lax.fori_loop(0, rows_scr.shape[0] // 2, pair, 0)


def lane_weight():
    lane = lax.broadcasted_iota(jnp.int32, (1, 2 * MY), 1)
    return jnp.where(lane % MY == 0, SCALE_INV, 2.0 * SCALE_INV).astype(jnp.float32)


def gelu_parts(v):
    cdf = 0.5 + 0.5 * lax.erf(v * root_half)
    bell = jnp.exp(v * v * -0.5)
    return v * cdf, cdf + v * bell * inv_root_tau


def mid_kernel(state_ref, other_ref, gout_ref, modes_ref, kron_ref, y_ref, x_ref, xt_ref, bias_ref,
               hot_ref, act_ref, gpre_ref, terms_ref, rows_scr, g_scr):
    step = pl.program_id(0)
    chans = gout_ref.shape[0]
    cols = gout_ref.shape[2]
    chunk = min(256, cols)

    @pl.when(step == 0)
    def _():
        expand_modes(modes_ref, x_ref, rows_scr, lane_weight())

    here = pl.ds(pl.multiple_of(step * TILE, TILE), TILE)
    rows = rows_scr[:, here, :].reshape(chans * TILE, 2 * MY)
    total = None
    for j in range(cols // chunk):
        lanes = slice(j * chunk, (j + 1) * chunk)
        cells = state_ref[:, :, lanes].reshape(-1, chunk)
        others = other_ref[:, :, lanes].reshape(-1, chunk)
        table = y_ref[:, lanes]
        pre = dot(kron_ref[0], cells) + dot(kron_ref[1], others) + dot(rows, table)
        bias = dot(bias_ref[...], hot_ref[0, :, lanes])
        parts = []
        for o in range(chans):
            v = pre[o * TILE:(o + 1) * TILE] + bias[o:o + 1]
            act, slope = gelu_parts(v)
            act_ref[o, :, lanes] = act.astype(jnp.bfloat16)
            grad = (gout_ref[o, :, lanes].astype(jnp.float32) * slope).astype(jnp.bfloat16)
            gpre_ref[o, :, lanes] = grad
            parts.append(grad)
        term = dot(jnp.concatenate(parts, 0), table, NT)
        total = term if total is None else total + term
    g_scr[:, here, :] = (total * lane_weight()).astype(jnp.bfloat16).reshape(chans, TILE, 2 * MY)

    @pl.when(step == pl.num_programs(0) - 1)
    def _():
        def one(o, carry):
            full = (dot(xt_ref[0], g_scr[o, :, :MY]) + dot(xt_ref[1], g_scr[o, :, MY:])).T
            wide = terms_ref.shape[-1]
            for g in range(terms_ref.shape[0]):
                terms_ref[g, o] = full[:, g * wide:(g + 1) * wide].astype(jnp.bfloat16)
            return carry

        lax.fori_loop(0, chans, one, 0)


def sums_kernel(state_ref, other_ref, gpre_ref, hot_ref, point_ref, bias_ref, acc, acc_b):
    step = pl.program_id(0)
    chans, tile, cols = gpre_ref.shape
    every = 2 * chans

    @pl.when(step == 0)
    def _():
        acc[...] = jnp.zeros_like(acc)
        acc_b[...] = jnp.zeros_like(acc_b)

    grad = gpre_ref[...]
    flat = grad.reshape(chans * tile, cols)
    acc[:, :chans * tile] += dot(flat, state_ref[...].reshape(chans * tile, cols), NT)
    acc[:, chans * tile:] += dot(flat, other_ref[...].reshape(chans * tile, cols), NT)
    col = grad.astype(jnp.float32).sum(axis=1)
    high = col.astype(jnp.bfloat16)
    low = (col - high.astype(jnp.float32)).astype(jnp.bfloat16)
    acc_b[...] += dot(high, hot_ref[0], NT) + dot(low, hot_ref[0], NT)

    @pl.when(step == pl.num_programs(0) - 1)
    def _():
        shape = (chans * tile, every * tile)
        row = lax.broadcasted_iota(jnp.int32, shape, 0) % tile
        lane = lax.broadcasted_iota(jnp.int32, shape, 1) % tile
        kept = jnp.where(row == lane, acc[...], 0.0)
        group = lax.broadcasted_iota(jnp.int32, (every * tile, every), 0) // tile
        which = lax.broadcasted_iota(jnp.int32, (every * tile, every), 1)
        ones = (group == which).astype(jnp.float32)
        summed = lax.dot_general(kept, ones, NN, precision=lax.Precision.HIGHEST,
                                 preferred_element_type=jnp.float32)
        point_ref[...] = summed.reshape(chans, tile, every).sum(axis=1) * SCALE_FWD
        bias_ref[...] = acc_b[...] * SCALE_FWD


def back_kernel(grad_ref, other_ref, modes_ref, kron_ref, y_ref, x_ref, out_ref, rows_scr):
    step = pl.program_id(0)
    chans, tile, cols = out_ref.shape
    chunk = min(256, cols)

    @pl.when(step == 0)
    def _():
        expand_modes(modes_ref, x_ref, rows_scr, SCALE_FWD)

    here = pl.ds(pl.multiple_of(step * TILE, TILE), TILE)
    rows = rows_scr[:, here, :].reshape(chans * TILE, 2 * MY)
    for j in range(cols // chunk):
        lanes = slice(j * chunk, (j + 1) * chunk)
        cells = grad_ref[:, :, lanes].reshape(-1, chunk)
        others = other_ref[:, :, lanes].reshape(-1, chunk)
        res = dot(kron_ref[0], cells) + dot(kron_ref[1], others) + dot(rows, y_ref[:, lanes])
        out_ref[:, :, lanes] = res.astype(jnp.bfloat16).reshape(chans, tile, chunk)


def whole(array):
    return pl.BlockSpec(array.shape, lambda *_: (0,) * array.ndim)


def call(kernel, name, grid, in_specs, out_specs, out_shape, scratch, cost):
    return pl.pallas_call(
        kernel, grid=grid, in_specs=in_specs, out_specs=out_specs, out_shape=out_shape,
        scratch_shapes=scratch, name=name,
        compiler_params=pltpu.CompilerParams(
            dimension_semantics=("arbitrary",), vmem_limit_bytes=VMEM_LIMIT
        ),
        cost_estimate=pl.CostEstimate(flops=cost[0], bytes_accessed=cost[1], transcendentals=0),
    )


def mix_modes(weight, spectrum):
    real_part = jnp.einsum("iokm,ikm->okm", weight[0], spectrum[0], precision="highest") - jnp.einsum(
        "iokm,ikm->okm", weight[1], spectrum[1], precision="highest"
    )
    imag_part = jnp.einsum("iokm,ikm->okm", weight[0], spectrum[1], precision="highest") + jnp.einsum(
        "iokm,ikm->okm", weight[1], spectrum[0], precision="highest"
    )
    return jnp.stack([real_part, imag_part])


def back_mix(weight, grad_modes):
    real_part = jnp.einsum("iokm,okm->ikm", weight[0], grad_modes[0], precision="highest") + jnp.einsum(
        "iokm,okm->ikm", weight[1], grad_modes[1], precision="highest"
    )
    imag_part = jnp.einsum("iokm,okm->ikm", weight[0], grad_modes[1], precision="highest") - jnp.einsum(
        "iokm,okm->ikm", weight[1], grad_modes[0], precision="highest"
    )
    return jnp.stack([real_part, imag_part])


def weight_grad(spectrum, grad_modes):
    s = spectrum[:, :, None]
    g = grad_modes[:, None]
    return jnp.stack([s[0] * g[0] + s[1] * g[1], s[0] * g[1] - s[1] * g[0]])


def bits_of(size):
    return range(size.bit_length() - 1)


def swap(array, axis, size, distance):
    return lax.ppermute(array, axis, [(i, i ^ distance) for i in range(size)])


def halve(array, axis, size, dim, beside):
    for b in bits_of(size):
        bit = (lax.axis_index(axis) >> b) & 1
        shape = array.shape
        split = array.reshape(shape[:dim] + (shape[dim] // 2, 2) + shape[dim + 1:])
        keep, send = (
            lax.dynamic_index_in_dim(split, which, dim + 1, False) for which in (bit, 1 - bit)
        )
        got = swap(send, axis, size, 1 << b)
        if b == 0 and beside is not None:
            got, beside = lax.optimization_barrier((got, beside))
        total = keep.astype(jnp.float32) + got.astype(jnp.float32)
        array = total.astype(jnp.bfloat16)
    return total, beside


def double(array, axis, size, dim):
    for b in reversed(bits_of(size)):
        first = ((lax.axis_index(axis) >> b) & 1) == 0
        got = swap(array, axis, size, 1 << b)
        both = jnp.stack([jnp.where(first, array, got), jnp.where(first, got, array)], dim + 1)
        shape = array.shape
        array = both.reshape(shape[:dim] + (2 * shape[dim],) + shape[dim + 1:])
    return array


def scatter_sum(terms, n_gx, n_gy, beside=(None, None)):
    chans, wide = terms.shape[1], terms.shape[3]
    total, one = halve(terms, "gy", n_gy, 0, beside[0])
    total = total.astype(jnp.bfloat16)[0].reshape(chans, n_gx, MY // n_gx, wide)
    total, two = halve(total, "gx", n_gx, 1, beside[1])
    total = total[:, 0]
    return jnp.stack([total[:, :, :wide // 2], total[:, :, wide // 2:]]), (one, two)


def gather_modes(modes, n_gx, n_gy):
    packed = jnp.concatenate([modes[0], modes[1]], -1)
    chans, _, wide = packed.shape
    packed = double(packed[:, None], "gx", n_gx, 1).reshape(1, chans, MY, wide)
    return double(packed, "gy", n_gy, 0)


def total_sum(array, n_gx, n_gy):
    for axis, size in (("gx", n_gx), ("gy", n_gy)):
        for b in bits_of(size):
            array = array + swap(array, axis, size, 1 << b)
    return array


def on_device(n_gx, n_gy, state_in, tile_class, class_bias, w_point, spec_weight, grad_out):
    chans, rows, cols = state_in.shape
    every = w_point.shape[0]
    gx_index = lax.axis_index("gx")
    gy_index = lax.axis_index("gy")
    col_index = lax.axis_index("col")
    bf16 = jnp.bfloat16
    y_all, x_all = host_tables(n_gy)
    y_table = lax.dynamic_slice_in_dim(jnp.asarray(y_all), gy_index * cols, cols, 1)
    x_table = lax.dynamic_slice_in_dim(jnp.asarray(x_all), gx_index * rows, rows, 1)
    x_table_t = lax.dynamic_slice_in_dim(jnp.asarray(x_all.transpose(0, 2, 1).copy()), gx_index * rows, rows, 2)
    state_other = swap(state_in, "col", 2, 1)
    first = col_index == 0
    w_rows = lax.dynamic_slice_in_dim(w_point, col_index * chans, chans, 0)
    w_cols = lax.dynamic_slice_in_dim(w_point, col_index * chans, chans, 1)
    same = jnp.eye(TILE, dtype=bf16)
    def kron_pair(weight):
        halves = weight.reshape(chans, 2, chans).transpose(1, 0, 2)
        halves = jnp.where(first, halves, halves[::-1])
        spread = halves[:, :, None, :, None] * same[None, None, :, None, :]
        return spread.reshape(2, chans * TILE, chans * TILE)

    kron_fwd, kron_bwd = kron_pair(w_rows), kron_pair(w_cols.T)
    hot = (
        jnp.repeat(tile_class, TILE, axis=1)[:, None, :]
        == (jnp.arange(2 * NCLASS, dtype=jnp.int32) % NCLASS)[None, :, None]
    ).astype(bf16)
    bias_own = lax.dynamic_slice_in_dim(class_bias, col_index * chans, chans, 1).T
    bias_high = bias_own.astype(bf16)
    bias_low = (bias_own - bias_high.astype(jnp.float32)).astype(bf16)
    bias_pair = jnp.concatenate([bias_high, bias_low], 1)

    steps = rows // TILE
    cells = rows * cols
    wide = 2 * MY
    block = pl.BlockSpec((chans, TILE, cols), lambda b: (0, b, 0))
    block_hot = pl.BlockSpec((1, 2 * NCLASS, cols), lambda b: (b, 0, 0))
    modes_shape = jax.ShapeDtypeStruct((n_gy, chans, MY, wide // n_gy), bf16)
    field_shape = jax.ShapeDtypeStruct((chans, rows, cols), bf16)
    rows_scratch = pltpu.VMEM((chans, rows, wide), bf16)

    terms = call(
        fwd_kernel, "forward_transform", (chans,),
        [pl.BlockSpec((1, rows, cols), lambda c: (c, 0, 0)), whole(y_table), whole(x_table)],
        pl.BlockSpec((n_gy, 1, MY, wide // n_gy), lambda c: (0, c, 0, 0)),
        modes_shape, [], (2 * chans * cells * wide, 2 * chans * cells),
    )(state_in, y_table, x_table)
    spectrum = scatter_sum(terms, n_gx, n_gy)[0] * SCALE_FWD
    spec_all = lax.all_gather(spectrum, "col", axis=1, tiled=True)
    weight_f = spec_weight.astype(jnp.float32)
    mixed = mix_modes(weight_f, spec_all).astype(bf16)
    mixed_all = gather_modes(mixed, n_gx, n_gy)

    act_out, grad_pre, grad_terms = call(
        mid_kernel, "layer_and_adjoint", (steps,),
        [block, block, block, whole(modes_shape), whole(kron_fwd), whole(y_table), whole(x_table),
         whole(x_table_t), whole(bias_pair), block_hot],
        [block, block, whole(modes_shape)],
        [field_shape, field_shape, modes_shape],
        [rows_scratch, rows_scratch],
        (2 * chans * cells * (2 * wide + every * TILE), 10 * chans * cells),
    )(state_in, state_other, grad_out, mixed_all, kron_fwd, y_table, x_table, x_table_t, bias_pair, hot)

    grad_other = swap(grad_pre, "col", 2, 1)
    def half_sums(part):
        start = part * (steps // 2)
        some = pl.BlockSpec((chans, TILE, cols), lambda b: (0, start + b, 0))
        some_hot = pl.BlockSpec((1, 2 * NCLASS, cols), lambda b: (start + b, 0, 0))
        point_sum, bias_sum = call(
            sums_kernel, f"weight_sums_{part}", (steps // 2,), [some, some, some, some_hot],
            [pl.BlockSpec((chans, every), lambda b: (0, 0)),
             pl.BlockSpec((chans, 2 * NCLASS), lambda b: (0, 0))],
            [jax.ShapeDtypeStruct((chans, every), jnp.float32),
             jax.ShapeDtypeStruct((chans, 2 * NCLASS), jnp.float32)],
            [pltpu.VMEM((chans * TILE, every * TILE), jnp.float32),
             pltpu.VMEM((chans, 2 * NCLASS), jnp.float32)],
            (chans * cells * every * TILE, 3 * chans * cells),
        )(state_in, state_other, grad_pre, hot)
        return jnp.concatenate([point_sum, bias_sum], 1)

    grad_modes, halves = scatter_sum(grad_terms, n_gx, n_gy, (half_sums(0), half_sums(1)))
    sums = halves[0] + halves[1]
    sums = total_sum(sums, n_gx, n_gy)
    own, other = sums[:, :chans], sums[:, chans:every]
    point_grad = jnp.concatenate(
        [jnp.where(first, own, other), jnp.where(first, other, own)], 1
    )
    bias_grad = sums[:, every:every + NCLASS].T

    input_terms = back_mix(weight_f, grad_modes)
    input_modes = lax.psum_scatter(input_terms, "col", scatter_dimension=1, tiled=True).astype(bf16)
    input_all = gather_modes(input_modes, n_gx, n_gy)
    spec_grad = weight_grad(spec_all, grad_modes)

    grad_in = call(
        back_kernel, "input_gradient", (steps,),
        [block, block, whole(modes_shape), whole(kron_bwd), whole(y_table), whole(x_table)],
        block, field_shape, [rows_scratch],
        (2 * chans * cells * (wide + every * TILE), 6 * chans * cells),
    )(grad_pre, grad_other, input_all, kron_bwd, y_table, x_table)
    return (act_out, grad_in, spec_grad, point_grad, bias_grad)


def solution(mesh):
    return jax.shard_map(
        functools.partial(on_device, mesh.shape["gx"], mesh.shape["gy"]),
        mesh=mesh,
        in_specs=(
            P(("groups", "col"), "gx", "gy"),
            P(("groups", "gx"), "gy"),
            P(),
            P(),
            P(None, None, "col", "gx", "gy"),
            P(("groups", "col"), "gx", "gy"),
        ),
        out_specs=(
            P(("groups", "col"), "gx", "gy"),
            P(("groups", "col"), "gx", "gy"),
            P("groups", None, "col", "gx", "gy"),
            P(("groups", "col"), None),
            P("groups", "col"),
        ),
        check_vma=False,
    )
```
